256 devices in a mesh: blk: 8 (over x_hi, y), dp: 32 (over x_lo, z, core).
Axes of the slice: x: 4 (x_hi: 2, x_lo: 2; x = x_hi * 2 + x_lo), y: 4, z: 8, core: 2. Of those that a mesh axis runs over, the one named last changes fastest.
Arguments:
- image_feats: bfloat16 [32, 1024, 1152], P('dp', 'blk'), may hold values from -6 to 6
- text_feats: bfloat16 [32, 1024, 1152], P('dp', 'blk'), may hold values from -6 to 6
- image_proj: bfloat16 [1152, 1152], replicated, may hold values from -0.1875 to 0.1875
- text_proj: bfloat16 [1152, 1152], replicated, may hold values from -0.1875 to 0.1875
- logit_scale: float32 [1], replicated, may hold values from 4 to 16
- logit_bias: float32 [1], replicated, may hold values from -6 to -2
Outputs:
- group_loss: float32 [32], P('dp')
- grad_image_proj: float32 [1152, 1152], P('dp')
- grad_text_proj: float32 [1152, 1152], P('dp')
- image_emb_grad: bfloat16 [32, 1024, 1152], P('dp', 'blk')
- text_emb_grad: bfloat16 [32, 1024, 1152], P('dp', 'blk')
The draws below stay inside these ranges and needn't reach their ends.
All inputs are finite; a program needn't handle non-finite values.
Results may differ from the reference program's by a relative error of at most 0.022.
Values may be sent and summed in bfloat16 or wider, within the bound.
No kernel may reach another device: no remote copies, remote signals or barrier semaphores. Data moves between devices by JAX's collectives and lax.ppermute only.
A program may use at most 128 MiB of HBM per device.

```python
import math
import jax
import jax.numpy as jnp
from jax import lax

D = 1152
E = 1152
GROUP_ROWS = 1024
GROUPS = 32


def raised(array, own_key, source, target, shards_of, factor):
    def block_of(dim):
        return (jnp.arange(array.shape[dim]) // (array.shape[dim] // shards_of)).reshape((-1,) + (1,) * (array.ndim - 1 - dim))

    near = jax.random.permutation(own_key, shards_of)[block_of(target)]
    other_side = (block_of(target) + shards_of // 2) % shards_of
    return jnp.where((block_of(source) == near) | (block_of(source) == other_side), factor * array, array)


def level_of(rng, shape, split, low, largest):
    def one(position, parts):
        steps = jax.random.uniform(jax.random.fold_in(jax.random.fold_in(rng, 6), position), (parts,), jnp.float32, low / len(split), largest / len(split))
        return jnp.repeat(jnp.exp(steps), shape[position] // parts).reshape((-1,) + (1,) * (len(shape) - position - 1))

    gain = one(*split[0])
    for cut in split[1:]:
        gain = gain * one(*cut)
    return gain


def normal_values(own_key, dims, spread, most, split=(), dtype=jnp.bfloat16):
    level = level_of(own_key, dims, split, -0.22, 0.18) if split else 1.0
    drawn = jax.random.normal(own_key, dims, jnp.float32) * spread * level
    return jnp.minimum(jnp.maximum(drawn, -most), most).astype(dtype)


def bell_draw_with(key, shape, spread, bound, split, heavy, held_as=jnp.bfloat16):
    array = spread * jax.random.normal(key, shape, jnp.float32)
    if split:
        array = array * level_of(key, shape, split, -0.22, 0.18)
    return jnp.clip(raised(array, jax.random.fold_in(key, 3), *heavy), -bound, bound).astype(held_as)


def setup_inputs(seed: int = 0) -> dict:
    key_of = jax.random.split(jax.random.key(seed), 7)
    image_feats = bell_draw_with(key_of[0], (GROUPS, GROUP_ROWS, D), 1.0, 6.0, ((0, 32), (1, 8)), (0, 2, 32, 2.75))
    text_feats = bell_draw_with(key_of[1], (GROUPS, GROUP_ROWS, D), 1.0, 6.0, ((0, 32), (1, 8)), (0, 2, 32, 2.75))
    image_proj = normal_values(key_of[2], (D, E), D ** -0.5, 0.1875)
    text_proj = normal_values(key_of[3], (D, E), D ** -0.5, 0.1875)
    logit_scale = jnp.clip(jnp.exp(jax.random.uniform(key_of[4], (1,), jnp.float32, math.log(4.0), math.log(16.0))), 4.0, 16.0)
    logit_bias = jnp.clip(jax.random.uniform(key_of[5], (1,), jnp.float32, -6.0, -2.0), -6.0, -2.0)
    return dict(image_feats=image_feats, text_feats=text_feats, image_proj=image_proj, text_proj=text_proj, logit_scale=logit_scale, logit_bias=logit_bias)


epsilon = 1e-06

def unit_rows(features, weight):
    projected = jnp.dot(features, weight, preferred_element_type=jnp.float32)
    inverse = lax.rsqrt(lax.optimization_barrier(jnp.sum(projected * projected, axis=-1, keepdims=True)) + epsilon)
    return (projected * inverse, inverse)

def back_unit(gradient, unit_vec, inverse):
    radial = lax.optimization_barrier(jnp.sum(unit_vec * gradient, axis=-1, keepdims=True))
    return ((gradient - unit_vec * radial) * inverse).astype(jnp.bfloat16)

def reference(image_feats, text_feats, image_proj, text_proj, logit_scale, logit_bias):
    logit_mult = logit_scale[0]
    offset = logit_bias[0]
    group_rows = image_feats.shape[1]

    def one_group(pair):
        image_rows, text_rows = pair
        image_unit, image_inv = unit_rows(image_rows, image_proj)
        text_unit, text_inv = unit_rows(text_rows, text_proj)
        image_emb = image_unit.astype(jnp.bfloat16)
        text_emb = text_unit.astype(jnp.bfloat16)
        logits = logit_mult * jnp.dot(image_emb, text_emb.T, preferred_element_type=jnp.float32) + offset
        diagonal = jnp.arange(group_rows)[:, None] == jnp.arange(group_rows)[None, :]
        target = jnp.where(diagonal, 1.0, -1.0).astype(jnp.float32)
        loss_value = -jnp.sum(jax.nn.log_sigmoid(target * logits)) / group_rows
        slopes = (-target * jax.nn.sigmoid(-target * logits)).astype(jnp.bfloat16)
        image_grad = logit_mult * jnp.dot(slopes, text_emb, preferred_element_type=jnp.float32)
        text_grad = logit_mult * jnp.dot(slopes.T, image_emb, preferred_element_type=jnp.float32)
        image_back = back_unit(image_grad, image_unit, image_inv)
        text_back = back_unit(text_grad, text_unit, text_inv)
        return (loss_value, image_grad.astype(jnp.bfloat16), text_grad.astype(jnp.bfloat16), image_back, text_back)
    group_loss, image_emb_grad, text_emb_grad, image_back, text_back = lax.map(one_group, (image_feats, text_feats))
    feature_width = image_feats.shape[2]
    embed_width = image_proj.shape[1]
    image_all = image_feats.reshape(-1, feature_width)
    text_all = text_feats.reshape(-1, feature_width)
    grad_image_proj = jnp.dot(image_all.T, image_back.reshape(-1, embed_width), preferred_element_type=jnp.float32)
    grad_text_proj = jnp.dot(text_all.T, text_back.reshape(-1, embed_width), preferred_element_type=jnp.float32)
    return (group_loss, grad_image_proj, grad_text_proj, image_emb_grad, text_emb_grad)
```

```python
import jax
import jax.numpy as jnp
from jax import lax
from jax.sharding import Mesh, PartitionSpec as P

epsilon = 1e-06
contract_rows = (((0,), (0,)), ((), ()))
contract_cols = (((1,), (1,)), ((), ()))
AXES = ("xh", "y", "xl", "z", "c")
XH, Y, XL, Z, C = 2, 4, 2, 8, 2
f32, bf16 = jnp.float32, jnp.bfloat16


def trade(x):
    return lax.ppermute(x, ("xh", "c"), [(1, 2), (2, 1)])


def other_core(x):
    return lax.ppermute(x, "c", [(0, 1), (1, 0)])


def from_y(x, k):
    return lax.ppermute(x, "y", [(i, (i + k) % Y) for i in range(Y)])


def gather(x, keep):
    own = jnp.where(keep, x, trade(x))
    return jnp.concatenate([own, from_y(own, 1), from_y(own, -1), from_y(own, 2)], axis=0)


def project(features, weight):
    pre = jnp.dot(features, weight, preferred_element_type=f32)
    inverse = lax.rsqrt(jnp.sum(pre * pre, axis=-1, keepdims=True) + epsilon)
    unit = pre * inverse
    return unit, inverse, unit.astype(bf16)


def on_device(image_feats, text_feats, image_proj, text_proj, logit_scale, logit_bias):
    c, y = lax.axis_index("c"), lax.axis_index("y")
    keep = lax.axis_index("xh") == c
    scale, bias = logit_scale[0], logit_bias[0]
    width = image_proj.shape[1]
    cols = width // Y
    rows = image_feats.shape[1] * Y
    own_rows = image_feats.shape[1]

    text = gather(text_feats[0], keep)
    image = gather(image_feats[0], keep)
    text_unit, text_inv, text_emb = project(text, text_proj)
    text_other = other_core(text_emb)
    image_unit, image_inv, image_emb = project(image, image_proj)
    text_all = jnp.concatenate([text_emb, text_other], axis=0)

    cosine = lax.dot_general(image_emb, text_all, contract_cols, preferred_element_type=f32)
    logits = scale * cosine + bias
    target = jnp.where(
        lax.broadcasted_iota(jnp.int32, logits.shape, 0)
        == lax.broadcasted_iota(jnp.int32, logits.shape, 1),
        1.0,
        -1.0,
    ).astype(f32)
    loss = -jnp.sum(jax.nn.log_sigmoid(target * logits)) / (rows * C)
    slopes = (-target * jax.nn.sigmoid(-target * logits)).astype(bf16)
    weighted = slopes.astype(f32) * cosine
    image_radial = scale * jnp.sum(weighted, axis=1, keepdims=True)
    text_radial = scale * jnp.sum(weighted, axis=0)[:, None]

    def cut(x):
        return lax.dynamic_slice_in_dim(x, y * cols, cols, axis=1)

    image_grad = scale * jnp.dot(slopes, cut(text_all), preferred_element_type=f32)
    text_part = scale * lax.dot_general(
        slopes, cut(image_emb), contract_rows, preferred_element_type=f32
    )
    text_grad = text_part[:rows] + other_core(text_part[rows:])
    text_radial = text_radial[:rows] + other_core(text_radial[rows:])
    image_back = ((image_grad - cut(image_unit) * image_radial) * image_inv).astype(bf16)
    text_back = ((text_grad - cut(text_unit) * text_radial) * text_inv).astype(bf16)
    image_term = lax.dot_general(image, image_back, contract_rows, preferred_element_type=f32)
    text_term = lax.dot_general(text, text_back, contract_rows, preferred_element_type=f32)
    term = jnp.concatenate([image_term, text_term], axis=1)
    term = term.reshape(XL * Z, C, -1, 2 * cols)
    give = lax.dynamic_index_in_dim(term, 1 - c, axis=1, keepdims=False).astype(bf16)
    mine = lax.dynamic_index_in_dim(term, c, axis=1, keepdims=False)
    mine = (mine + other_core(give).astype(f32)).astype(bf16)
    got = lax.all_to_all(mine, ("xl", "z"), 0, 0)
    summed = jnp.sum(got.astype(f32), axis=0).astype(bf16)
    spread = lax.all_to_all(
        jnp.broadcast_to(summed[None], (XH * Y,) + summed.shape), ("xh", "y"), 0, 0
    )
    spread = spread.astype(f32)
    spread = spread[:Y] + spread[Y:]
    grads = [
        jnp.concatenate([spread[i, :, s * cols : (s + 1) * cols] for i in range(Y)], axis=1)
        for s in range(2)
    ]

    image_out = scale * jnp.dot(slopes[:own_rows], text_all, preferred_element_type=f32)
    parts = [
        lax.dot_general(
            slopes[:, i : i + own_rows], image_emb, contract_rows, preferred_element_type=f32
        )
        for i in (0, rows)
    ]
    text_out = scale * (parts[0] + other_core(parts[1]))
    outs = jnp.concatenate([image_out.astype(bf16), text_out.astype(bf16)], axis=0)
    loss = jnp.broadcast_to(loss, (8, 128))
    loss = loss + other_core(loss)
    outs = jnp.where(keep, outs, trade(outs))
    loss = jnp.where(keep, loss, trade(loss))
    return (
        loss[0, :1],
        grads[0],
        grads[1],
        outs[:own_rows][None],
        outs[own_rows:][None],
    )


def solution(mesh):
    fine = Mesh(mesh.devices.reshape(XH, Y, XL, Z, C), AXES)
    dp, blk = ("xl", "z", "c"), ("xh", "y")
    in_specs = (P(dp, blk, None), P(dp, blk, None), P(), P(), P(), P())
    out_specs = (P(dp), P(dp, None), P(dp, None), P(dp, blk, None), P(dp, blk, None))
    return jax.shard_map(
        on_device, mesh=fine, in_specs=in_specs, out_specs=out_specs, check_vma=False
    )
```

```python
import jax
import jax.numpy as jnp
from jax import lax
from jax.experimental import pallas as pl
from jax.experimental.pallas import tpu as pltpu
from jax.sharding import Mesh, PartitionSpec as P

epsilon = 1e-06
AXES = ("xh", "y", "xl", "z", "c")
XH, Y, XL, Z, C = 2, 4, 2, 8, 2
WIDE, SLIM = 256, 128
f32, bf16 = jnp.float32, jnp.bfloat16


def trade(x):
    return lax.ppermute(x, ("xh", "c"), [(0, 0), (1, 2), (2, 1), (3, 3)])


def other_core(x):
    return lax.ppermute(x, "c", [(0, 1), (1, 0)])


def from_y(x, k):
    return lax.ppermute(x, "y", [(i, (i + k) % Y) for i in range(Y)])


def gather(own):
    return own, from_y(own, 1), from_y(own, -1), from_y(own, 2)


def dot(a, b):
    return lax.dot_general(a, b, (((1,), (0,)), ((), ())), preferred_element_type=f32)


def dot_cols(a, b):
    return lax.dot_general(a, b, (((1,), (1,)), ((), ())), preferred_element_type=f32)


def dot_rows(a, b):
    return lax.dot_general(a, b, (((0,), (0,)), ((), ())), preferred_element_type=f32)


def image_start(y):
    return pl.multiple_of(y * WIDE + jnp.where(y > 0, SLIM, 0), SLIM)


def text_start(y):
    return pl.multiple_of(y * WIDE, WIDE)


def join_and_project(pieces, weight, cat, emb, unit, inv):
    n = pieces[0].shape[0]
    for i, piece in enumerate(pieces):
        cat[i * n : (i + 1) * n, :] = piece[...]
    rows = cat.shape[0]
    step = rows // 2
    for r in range(0, rows, step):
        pre = dot(cat[r : r + step, :], weight[...])
        inverse = lax.rsqrt(jnp.sum(pre * pre, axis=1, keepdims=True) + epsilon)
        value = pre * inverse
        unit[r : r + step, :] = value
        emb[r : r + step, :] = value.astype(bf16)
        inv[r : r + step, :] = jnp.broadcast_to(inverse, (step, inv.shape[1]))


def text_kernel(ids, t0, t1, t2, t3, weight, cat, emb, window, inv, unit):
    join_and_project((t0, t1, t2, t3), weight, cat, emb, unit, inv)
    y = ids[0]
    window[:, :WIDE] = unit[:, pl.ds(text_start(y), WIDE)]
    window[:, WIDE:] = unit[:, unit.shape[1] - SLIM :]


def image_kernel(ids, i0, i1, i2, i3, weight, cat, emb, window, inv, unit):
    join_and_project((i0, i1, i2, i3), weight, cat, emb, unit, inv)
    y = ids[0]
    window[:, :WIDE] = unit[:, pl.ds(image_start(y), WIDE)]
    window[:, WIDE:] = unit[:, WIDE : WIDE + SLIM]


def slope_kernel(
    ids, scal, emb, own, other, slopes, radial, text_radial, give, give_out, loss
):
    y = ids[0]
    scale, bias = scal[0], scal[1]
    rows = emb.shape[0]
    embedded = emb[...]
    lost = jnp.zeros((8, WIDE), f32)
    along = jnp.zeros((rows, WIDE), f32)
    for j in range(2 * rows // WIDE):
        mine = j * WIDE < rows
        side, at = (own, j * WIDE) if mine else (other, j * WIDE - rows)
        cosine = dot_cols(embedded, side[at : at + WIDE, :])
        logits = scale * cosine + bias
        if mine:
            same = (
                lax.broadcasted_iota(jnp.int32, logits.shape, 0)
                == lax.broadcasted_iota(jnp.int32, logits.shape, 1) + at
            )
            logits = jnp.where(same, -logits, logits)
        small = jnp.exp(-jnp.abs(logits))
        term = jnp.maximum(logits, 0.0) + jnp.log1p(small)
        lost = lost + jnp.sum(term.reshape(rows // 8, 8, WIDE), axis=0)
        slope = jnp.where(logits >= 0, 1.0, small) / (1.0 + small)
        if mine:
            slope = jnp.where(same, -slope, slope)
        slope = slope.astype(bf16)
        slopes[:, j * WIDE : (j + 1) * WIDE] = slope
        weighted = slope.astype(f32) * cosine
        along = along + weighted
        down = jnp.sum(weighted, axis=0, keepdims=True)
        down = jnp.transpose(jnp.broadcast_to(down, (SLIM, WIDE)))
        if mine:
            text_radial[at : at + WIDE, :] = down
        else:
            give[at : at + WIDE, WIDE + SLIM :] = down
    radial[...] = jnp.broadcast_to(jnp.sum(along, axis=1, keepdims=True), radial.shape)
    loss[...] = jnp.broadcast_to(jnp.sum(lost, keepdims=True), loss.shape)
    give[:, :WIDE] = dot_rows(slopes[:, rows:], emb[:, pl.ds(text_start(y), WIDE)])

    @pl.when(y == Y - 1)
    def _():
        give[:, WIDE : WIDE + SLIM] = dot_rows(slopes[:, rows:], emb[:, emb.shape[1] - SLIM :])

    @pl.when(y != Y - 1)
    def _():
        give[:, WIDE : WIDE + SLIM] = jnp.zeros((rows, SLIM), f32)

    give_out[...] = dot_rows(slopes[:, rows : rows + give_out.shape[0]], embedded)


def wide(x, n):
    return jnp.concatenate([x] * (n // x.shape[1]), axis=1)


def back(grad, window, radial, inv):
    n = grad.shape[1]
    return ((grad - window * wide(radial, n)) * wide(inv, n)).astype(bf16)


def grad_kernel(
    ids, scal, cat, emb, window, inv, slopes, radial, own, other,
    term, part, out, part_out,
):
    y = ids[0]
    scale = scal[0]
    rows = cat.shape[0]
    n = out.shape[0]

    def columns(cols, at, size):
        grad = dot(slopes[:, :rows], own[:, cols]) + dot(slopes[:, rows:], other[:, cols])
        grad = back(scale * grad, window[:, at : at + size], scale * radial[...], inv[...])
        term[:, at : at + size] = dot_rows(cat[...], grad)

    columns(pl.ds(image_start(y), WIDE), 0, WIDE)
    part[:, :WIDE] = dot_rows(slopes[:, :rows], emb[:, pl.ds(text_start(y), WIDE)])

    @pl.when(y == 0)
    def _():
        columns(slice(WIDE, WIDE + SLIM), WIDE, SLIM)

    @pl.when(y == Y - 1)
    def _():
        part[:, WIDE:] = dot_rows(slopes[:, :rows], emb[:, emb.shape[1] - SLIM :])

    @pl.when(y != Y - 1)
    def _():
        part[:, WIDE:] = jnp.zeros((rows, SLIM), f32)

    out[...] = (scale * (dot(slopes[:n, :rows], own[...]) + dot(slopes[:n, rows:], other[...]))).astype(bf16)
    part_out[...] = dot_rows(slopes[:, :n], emb[...])


def sum_kernel(
    ids, scal, cat, window, inv, text_radial, part, got, part_out, got_out, image_term,
    give, keep, out, term,
):
    y, c = ids[0], ids[1]
    scale = scal[0]
    grad = scale * (part[...] + got[:, : WIDE + SLIM])
    radial = scale * (text_radial[...] + got[:, WIDE + SLIM :])
    grad = back(grad, window[...], radial, inv[...])
    term[:, :WIDE] = dot_rows(cat[...], grad[:, :WIDE])

    @pl.when(y == Y - 1)
    def _():
        term[:, WIDE:] = dot_rows(cat[...], grad[:, WIDE:])

    @pl.when(y == 0)
    def _():
        term[:, WIDE:] = image_term[:, WIDE:]

    @pl.when((y != 0) & (y != Y - 1))
    def _():
        term[:, WIDE:] = jnp.zeros((term.shape[0], SLIM), f32)

    first = c == 0
    half = keep.shape[1]
    for k in range(keep.shape[0]):
        for source, at, size in ((image_term, 0, WIDE), (term, WIDE, WIDE + SLIM)):
            low = source[2 * half * k : 2 * half * k + half, :size]
            high = source[2 * half * k + half : 2 * half * (k + 1), :size]
            keep[k, :, at : at + size] = jnp.where(first, low, high)
            give[k, :, at : at + size] = jnp.where(first, high, low).astype(bf16)
    out[...] = (scale * (part_out[...] + got_out[...])).astype(bf16)


def call(kernel, outs, scratch=(), macs=0):
    def in_vmem(x):
        return pl.BlockSpec(memory_space=pltpu.SMEM if x.ndim == 1 else pltpu.VMEM)

    def run(*args):
        return pl.pallas_call(
            kernel,
            out_shape=[jax.ShapeDtypeStruct(s, d) for s, d in outs],
            in_specs=[in_vmem(a) for a in args],
            out_specs=[pl.BlockSpec(memory_space=pltpu.VMEM) for _ in outs],
            scratch_shapes=list(scratch),
            compiler_params=pltpu.CompilerParams(vmem_limit_bytes=40 * 2**20),
            cost_estimate=pl.CostEstimate(flops=2 * macs, bytes_accessed=0, transcendentals=0),
        )(*args)

    return run


def on_device(image_feats, text_feats, image_proj, text_proj, logit_scale, logit_bias):
    c, y = lax.axis_index("c"), lax.axis_index("y")
    ids = jnp.stack([y, c]).astype(jnp.int32)
    scal = jnp.concatenate([logit_scale, logit_bias])
    n, depth = image_feats.shape[1:]
    width = image_proj.shape[1]
    rows = n * Y

    text_own, image_own = trade(text_feats[0]), trade(image_feats[0])
    text = gather(text_own)
    image = gather(image_own)
    projected = [
        ((rows, depth), bf16), ((rows, width), bf16), ((rows, WIDE + SLIM), f32), ((rows, SLIM), f32),
    ]
    unit = [pltpu.VMEM((rows, width), f32)]
    macs = 20 * rows * depth * width
    text_cat, text_emb, text_window, text_inv = call(text_kernel, projected, unit, macs)(ids, *text, text_proj)
    text_other = other_core(text_emb)
    image_cat, image_emb, image_window, image_inv = call(image_kernel, projected, unit, macs)(ids, *image, image_proj)
    slopes, image_radial, text_radial, give, give_out, loss = call(
        slope_kernel,
        [
            ((rows, C * rows), bf16), ((rows, SLIM), f32), ((rows, SLIM), f32),
            ((rows, WIDE + 2 * SLIM), f32), ((n, width), f32), ((8, SLIM), f32),
        ],
    )(ids, scal, image_emb, text_emb, text_other)
    got, got_out = other_core(give), other_core(give_out)
    image_term, part, image_out, part_out = call(
        grad_kernel,
        [((depth, WIDE + SLIM), f32), ((rows, WIDE + SLIM), f32), ((n, width), bf16), ((n, width), f32)],
    )(ids, scal, image_cat, image_emb, image_window, image_inv, slopes, image_radial, text_emb, text_other)
    each = depth // (XL * Z * C)
    wide_term = 2 * WIDE + SLIM
    give, keep, text_out = call(
        sum_kernel,
        [((XL * Z, each, wide_term), bf16), ((XL * Z, each, wide_term), f32), ((n, width), bf16)],
        [pltpu.VMEM((depth, WIDE + SLIM), f32)],
    )(
        ids, scal, text_cat, text_window, text_inv, text_radial, part, got, part_out, got_out, image_term,
    )
    mine = (keep + other_core(give).astype(f32)).astype(bf16)
    arrived = lax.all_to_all(mine, ("xl", "z"), 0, 0)
    summed = jnp.sum(arrived.astype(f32), axis=0).astype(bf16)
    spread = lax.all_to_all(
        jnp.broadcast_to(summed[None], (XH * Y,) + summed.shape), ("xh", "y"), 0, 0
    )
    spread = spread.astype(f32)
    spread = spread[:Y] + spread[Y:]
    image_grad = [spread[0, :, :WIDE], spread[0, :, 2 * WIDE :]] + [spread[i, :, :WIDE] for i in range(1, Y)]
    text_grad = [spread[i, :, WIDE : 2 * WIDE] for i in range(Y)] + [spread[Y - 1, :, 2 * WIDE :]]

    outs = trade(jnp.concatenate([image_out, text_out], axis=0))
    loss = trade(loss + other_core(loss)) / (rows * C)
    return (
        loss[0, :1],
        jnp.concatenate(image_grad, axis=1),
        jnp.concatenate(text_grad, axis=1),
        outs[:n][None],
        outs[n:][None],
    )


def solution(mesh):
    fine = Mesh(mesh.devices.reshape(XH, Y, XL, Z, C), AXES)
    dp, blk = ("xl", "z", "c"), ("xh", "y")
    in_specs = (P(dp, blk, None), P(dp, blk, None), P(), P(), P(), P())
    out_specs = (P(dp), P(dp, None), P(dp, None), P(dp, blk, None), P(dp, blk, None))
    return jax.shard_map(
        on_device, mesh=fine, in_specs=in_specs, out_specs=out_specs, check_vma=False
    )
```

```python
import jax
import jax.numpy as jnp
from jax import lax
from jax.experimental import pallas as pl
from jax.experimental.pallas import tpu as pltpu
from jax.sharding import Mesh, PartitionSpec as P

epsilon = 1e-06
AXES = ("xh", "y", "xl", "z", "c")
XH, Y, XL, Z, C = 2, 4, 2, 8, 2
WIDE, SLIM, PACK, TERMS = 256, 128, 192, 16
f32, bf16 = jnp.float32, jnp.bfloat16


def trade(x):
    return lax.ppermute(x, ("xh", "c"), [(0, 0), (1, 2), (2, 1), (3, 3)])


def other_core(x):
    return lax.ppermute(x, "c", [(0, 1), (1, 0)])


def from_y(x, k):
    return lax.ppermute(x, "y", [(i, (i + k) % Y) for i in range(Y)])


def gather(own):
    return own, from_y(own, 1), from_y(own, -1), from_y(own, 2)


def dot(a, b):
    return lax.dot_general(a, b, (((1,), (0,)), ((), ())), preferred_element_type=f32)


def dot_cols(a, b):
    return lax.dot_general(a, b, (((1,), (1,)), ((), ())), preferred_element_type=f32)


def image_start(y):
    return pl.multiple_of(y * WIDE + jnp.where(y > 0, SLIM, 0), SLIM)


def text_start(y):
    return pl.multiple_of(y * WIDE, WIDE)


def join(parts, whole):
    at = 0
    for part in parts:
        whole[at : at + part.shape[0], :] = part[...]
        at += part.shape[0]


def finish(pre, square, emb, window, inv, unit, start, extra):
    inverse = lax.rsqrt(square + epsilon)
    value = pre * inverse
    unit[...] = value
    emb[...] = value.astype(bf16)
    inv[...] = jnp.broadcast_to(inverse, inv.shape)
    window[:, :WIDE] = unit[:, pl.ds(start, WIDE)]
    window[:, WIDE:] = unit[:, extra : extra + SLIM]


def text_kernel(ids, *refs):
    *pieces, weight, turned, emb, window, inv, joined, unit, held, arrived = refs
    copy = pltpu.make_async_copy(weight, held, arrived)
    copy.start()
    join(pieces, joined)
    features = joined[...]
    turned[...] = features.T
    copy.wait()
    pre = dot(features, held[...])
    square = jnp.sum(pre * pre, axis=1, keepdims=True)
    finish(pre, square, emb, window, inv, unit, text_start(ids[0]), weight.shape[1] - SLIM)


def image_kernel(ids, *refs):
    *pieces, weight, turned, emb, window, inv, joined, unit = refs
    join(pieces, joined)
    features = joined[...]
    pre = dot(features, weight[...])
    square = jnp.sum(pre * pre, axis=1, keepdims=True)
    finish(pre, square, emb, window, inv, unit, image_start(ids[0]), WIDE)
    turned[...] = features.T


def fold(x, combine):
    while x.shape[0] > 8:
        half = x.shape[0] // 2
        x = combine(x[:half], x[half:])
    return x


def stack(refs):
    return jnp.concatenate([ref[...] for ref in refs], axis=0)


def slope_kernel(
    ids, scal, far, weight, early, own, other,
    emb, turned, window, inv, slopes, slopes_turned, radial, text_radial, give, loss,
    late, joined, unit,
):
    y = ids[0]
    scale, bias = scal[0], scal[1]
    image_kernel(ids, far, weight, turned, late, window, inv, joined, unit)
    rows = emb.shape[0]
    join((early, late), emb)
    embedded = emb[...]
    lost = jnp.zeros((8, WIDE), f32)
    along = [jnp.zeros((WIDE, WIDE), f32) for _ in range(0, rows, WIDE)]
    for j in reversed(range(0, 2 * rows, WIDE)):
        mine = j < rows
        side, at = (own, j) if mine else (other, j - rows)
        cosines = dot_cols(embedded, side[at : at + WIDE, :])
        down = jnp.zeros((8, WIDE), f32)
        for i in range(0, rows, WIDE):
            cosine = cosines[i : i + WIDE]
            logits = scale * cosine + bias
            diagonal = mine and i == at
            if diagonal:
                same = lax.broadcasted_iota(jnp.int32, logits.shape, 0) == lax.broadcasted_iota(
                    jnp.int32, logits.shape, 1
                )
                logits = jnp.where(same, -logits, logits)
            small = jnp.exp(-jnp.abs(logits))
            whole = 1.0 + small
            slope = jnp.where(logits >= 0, 1.0, small) * pl.reciprocal(whole, approx=True)
            if diagonal:
                slope = jnp.where(same, -slope, slope)
            slope = slope.astype(bf16)
            lost = lost + fold(jnp.maximum(logits, 0.0), jnp.add) + jnp.log(fold(whole, jnp.multiply))
            slopes[i : i + WIDE, j : j + WIDE] = slope
            slopes_turned[j : j + WIDE, i : i + WIDE] = slope.T
            weighted = slope.astype(f32) * cosine
            along[i // WIDE] = along[i // WIDE] + weighted
            down = down + fold(weighted, jnp.add)
        down = jnp.sum(down, axis=0, keepdims=True)
        down = jnp.transpose(jnp.broadcast_to(down, (SLIM, WIDE)))
        if mine:
            text_radial[at : at + WIDE, :] = down
        else:
            give[at : at + WIDE, WIDE + SLIM :] = down
    for i, part in enumerate(along):
        part = jnp.sum(part, axis=1, keepdims=True)
        radial[i * WIDE : (i + 1) * WIDE, :] = jnp.broadcast_to(part, (WIDE, SLIM))
    loss[...] = jnp.broadcast_to(jnp.sum(lost, keepdims=True), loss.shape)
    give[:, :WIDE] = dot(slopes_turned[rows:, :], emb[:, pl.ds(text_start(y), WIDE)])

    @pl.when(y == Y - 1)
    def _():
        give[:, WIDE : WIDE + SLIM] = dot(slopes_turned[rows:, :], emb[:, emb.shape[1] - SLIM :])

    @pl.when(y != Y - 1)
    def _():
        give[:, WIDE : WIDE + SLIM] = jnp.zeros((rows, SLIM), f32)


def wide(x, n):
    return jnp.concatenate([x] * (n // x.shape[1]), axis=1)


def back(grad, window, radial, inv):
    n = grad.shape[1]
    return ((grad - window * wide(radial, n)) * wide(inv, n)).astype(bf16)


def outer(turned, grad):
    return dot(jnp.concatenate([part[...] for part in turned], axis=1), grad)


def grad_kernel(
    ids, scal, f0, f1, w0, w1, v0, v1, emb, slopes, slopes_turned, radial, own, other,
    term, part,
):
    y = ids[0]
    scale = scal[0]
    rows = emb.shape[0]
    window, inv = stack((w0, w1)), stack((v0, v1))

    def columns(cols, at, size):
        grad = scale * (dot(slopes[:, :rows], own[:, cols]) + dot(slopes[:, rows:], other[:, cols]))
        grad = back(grad, window[:, at : at + size], scale * radial[...], inv)
        term[:, at : at + size] = outer((f0, f1), grad)

    columns(pl.ds(image_start(y), WIDE), 0, WIDE)
    part[:, :WIDE] = dot(slopes_turned[:rows, :], emb[:, pl.ds(text_start(y), WIDE)])

    @pl.when(y == 0)
    def _():
        columns(slice(WIDE, WIDE + SLIM), WIDE, SLIM)

    @pl.when(y == Y - 1)
    def _():
        part[:, WIDE:] = dot(slopes_turned[:rows, :], emb[:, emb.shape[1] - SLIM :])

    @pl.when(y != Y - 1)
    def _():
        part[:, WIDE:] = jnp.zeros((rows, SLIM), f32)


def sum_kernel(
    ids, scal, turned, window, inv, text_radial, part, got, image_term,
    give, keep, token, term,
):
    y, c = ids[0], ids[1]
    scale = scal[0]
    grad = scale * (part[...] + got[:, : WIDE + SLIM])
    radial = scale * (text_radial[...] + got[:, WIDE + SLIM :])
    grad = back(grad, window[...], radial, inv[...])
    term[:, :WIDE] = dot(turned[...], grad[:, :WIDE])

    @pl.when(y == Y - 1)
    def _():
        term[:, WIDE:] = dot(turned[...], grad[:, WIDE:])

    @pl.when(y == 0)
    def _():
        term[:, WIDE:] = image_term[:, WIDE:]

    @pl.when((y != 0) & (y != Y - 1))
    def _():
        term[:, WIDE:] = jnp.zeros((term.shape[0], SLIM), f32)

    token[...] = jnp.zeros(token.shape, f32)
    for k in range(XL * Z):
        for core, out in ((c, keep), (1 - c, give)):
            packed = pack(image_term, term, k, core).astype(out.dtype)
            out[k] = packed


def pack(image_term, term, k, core):
    tiles = [(image_term, 0), (image_term, SLIM), (term, 0), (term, SLIM), (term, 2 * SLIM)]
    base = 72 * k
    whole = pl.ds(pl.multiple_of(base + 40 * core, 8), 32)
    parts = [source[whole, col : col + SLIM] for source, col in tiles]
    split = [source[base + 32 : base + 40, col : col + SLIM] for source, col in tiles]
    owned = lax.broadcasted_iota(jnp.int32, (8, SLIM), 0) // 4 == core
    parts += [jnp.where(owned, split[i], pltpu.roll(split[i + 1], 4, 0)) for i in (0, 2)]
    parts += [split[4], jnp.zeros((8, SLIM), f32)]
    return jnp.concatenate(parts, axis=0)


def add_kernel(keep, got, mine, token):
    token[...] = jnp.zeros(token.shape, f32)
    mine[...] = (keep[...] + got[...].astype(f32)).astype(bf16)


def spread_kernel(parts, spread):
    summed = jnp.sum(parts[...].astype(f32), axis=0).astype(bf16)
    for i in range(spread.shape[0]):
        spread[i] = summed


def unpack_kernel(ids, spread, outs, image_out, text_out, loss, image_emb_out, text_emb_out):
    core = ids[1]
    n = image_emb_out.shape[1]
    image_emb_out[0] = outs[:n, :]
    text_emb_out[0] = outs[n : 2 * n, :]
    loss[0] = jnp.sum(outs[2 * n :, :SLIM].astype(f32)[:, :1])

    def place(c):
        for y in range(Y):
            rows = spread[y].astype(f32) + spread[Y + y].astype(f32)
            for tile in range(5):
                if tile < 2:
                    out, col = image_out, 2 * y + tile + (1 if y > 0 else 0)
                elif tile < 4:
                    out, col = text_out, 2 * y + tile - 2
                elif y == 0:
                    out, col = image_out, 2
                elif y == Y - 1:
                    out, col = text_out, 2 * Y
                else:
                    continue
                cols = slice(col * SLIM, (col + 1) * SLIM)
                shared = 160 + 8 * (tile // 2) + 4 * (c if tile % 2 == 0 else 1 - c)
                out[4 * c : 4 * c + 32, cols] = rows[32 * tile : 32 * tile + 32]
                out[32 * (1 - c) : 32 * (1 - c) + 4, cols] = rows[shared : shared + 4]

    for c in range(C):
        pl.when(core == c)(lambda c=c: place(c))


def rest_kernel(slopes_turned, emb, loss, after, give):
    del after
    n = give.shape[0] - 8
    rows = emb.shape[0]
    give[:n, :] = dot(slopes_turned[rows : rows + n, :], emb[...])
    give[n:, :] = jnp.broadcast_to(loss[:, :1], (8, give.shape[1]))


def out_kernel(scal, slopes, slopes_turned, emb, own, other, loss, got, after, out):
    del after
    scale = scal[0]
    n = got.shape[0] - 8
    rows = emb.shape[0]
    out[:n, :] = (scale * (dot(slopes[:n, :rows], own[...]) + dot(slopes[:n, rows:], other[...]))).astype(bf16)
    out[n : 2 * n, :] = (scale * (dot(slopes_turned[:n, :], emb[...]) + got[:n, :])).astype(bf16)
    left = (loss[:1, :1] + got[n : n + 1, :1]) * (1.0 / (C * rows))
    row = lax.broadcasted_iota(jnp.int32, (TERMS, out.shape[1]), 0)
    terms = jnp.zeros(row.shape, f32)
    for i in range(3):
        term = left.astype(bf16).astype(f32)
        terms = jnp.where(row == i, term, terms)
        left = left - term
    out[2 * n :, :] = terms.astype(bf16)


def call(kernel, outs, scratch=(), macs=0, far=None):
    def space(i, x):
        if i == far:
            return pltpu.HBM
        return pltpu.SMEM if x.ndim == 1 else pltpu.VMEM

    def run(*args):
        return pl.pallas_call(
            kernel,
            out_shape=[jax.ShapeDtypeStruct(s, d) for s, d in outs],
            in_specs=[pl.BlockSpec(memory_space=space(i, a)) for i, a in enumerate(args)],
            out_specs=[pl.BlockSpec(memory_space=pltpu.SMEM if len(s) == 1 else pltpu.VMEM) for s, _ in outs],
            scratch_shapes=list(scratch),
            compiler_params=pltpu.CompilerParams(vmem_limit_bytes=16 * 2**20),
            cost_estimate=pl.CostEstimate(flops=2 * macs, bytes_accessed=0, transcendentals=0),
        )(*args)

    return run


def on_device(image_feats, text_feats, image_proj, text_proj, logit_scale, logit_bias):
    c, y = lax.axis_index("c"), lax.axis_index("y")
    ids = jnp.stack([y, c]).astype(jnp.int32)
    scal = jnp.concatenate([logit_scale, logit_bias])
    n, depth = image_feats.shape[1:]
    width = image_proj.shape[1]
    rows = n * Y
    macs = 20 * rows * depth * width

    def projected(count):
        return [((depth, count), bf16), ((count, width), bf16), ((count, WIDE + SLIM), f32), ((count, SLIM), f32)]

    def scratch(count):
        return [pltpu.VMEM((count, depth), bf16), pltpu.VMEM((count, width), f32)]

    text = gather(trade(text_feats[0]))
    image = gather(trade(image_feats[0]))
    streams = [pltpu.VMEM((depth, width), bf16), pltpu.SemaphoreType.DMA]
    text_turned, text_emb, text_window, text_inv = call(
        text_kernel, projected(rows), scratch(rows) + streams, macs, len(text) + 1
    )(ids, *text, pltpu.with_memory_space_constraint(text_proj, pltpu.HBM))
    text_other = other_core(text_emb)
    turned_a, early, window_a, inv_a = call(image_kernel, projected(3 * n), scratch(3 * n), macs)(
        ids, *image[:3], image_proj
    )
    turned, _, window, inv = projected(n)
    emb, turned_b, window_b, inv_b, slopes, slopes_turned, radial, text_radial, give, loss = call(
        slope_kernel,
        [
            ((rows, width), bf16), turned, window, inv,
            ((rows, C * rows), bf16), ((C * rows, rows), bf16), ((rows, SLIM), f32), ((rows, SLIM), f32),
            ((rows, WIDE + 2 * SLIM), f32), ((8, SLIM), f32),
        ],
        [pltpu.VMEM((n, width), bf16)] + scratch(n),
        macs,
    )(ids, scal, *image[3:], image_proj, early, text_emb, text_other)
    got = other_core(give)
    image_term, part = call(grad_kernel, [((depth, WIDE + SLIM), f32), ((rows, WIDE + SLIM), f32)], (), macs)(
        ids, scal, turned_a, turned_b, window_a, window_b, inv_a, inv_b, emb, slopes, slopes_turned,
        radial, text_emb, text_other,
    )
    packed = (XL * Z, PACK, SLIM)
    give, keep, token = call(
        sum_kernel,
        [(packed, bf16), (packed, f32), ((8, SLIM), f32)],
        [pltpu.VMEM((depth, WIDE + SLIM), f32)],
    )(ids, scal, text_turned, text_window, text_inv, text_radial, part, got, image_term)
    mine, behind = call(add_kernel, [(packed, bf16), ((8, SLIM), f32)])(keep, other_core(give))
    arrived = lax.all_to_all(mine, ("xl", "z"), 0, 0)
    (spread,) = call(spread_kernel, [((XH * Y, PACK, SLIM), bf16)])(arrived)
    spread = lax.all_to_all(spread, ("xh", "y"), 0, 0)
    (give_rest,) = call(rest_kernel, [((n + 8, width), f32)], (), macs)(slopes_turned, emb, loss, token)
    (outs,) = call(out_kernel, [((2 * n + TERMS, width), bf16)], (), macs)(
        scal, slopes, slopes_turned, emb, text_emb, text_other, loss, other_core(give_rest), behind
    )
    outs = trade(outs)
    grad = (depth // (XL * Z * C), width), f32
    image_grad, text_grad, total, image_out, text_out = call(
        unpack_kernel, [grad, grad, ((1,), f32), ((1, n, width), bf16), ((1, n, width), bf16)]
    )(ids, spread, outs)
    return total, image_grad, text_grad, image_out, text_out


def solution(mesh):
    fine = Mesh(mesh.devices.reshape(XH, Y, XL, Z, C), AXES)
    dp, blk = ("xl", "z", "c"), ("xh", "y")
    in_specs = (P(dp, blk, None), P(dp, blk, None), P(), P(), P(), P())
    out_specs = (P(dp), P(dp, None), P(dp, None), P(dp, blk, None), P(dp, blk, None))
    return jax.shard_map(
        on_device, mesh=fine, in_specs=in_specs, out_specs=out_specs, check_vma=False
    )
```

```python
import jax
import jax.numpy as jnp
from jax import lax
from jax.experimental import pallas as pl
from jax.experimental.pallas import tpu as pltpu
from jax.sharding import Mesh, PartitionSpec as P

epsilon = 1e-06
LOG2_E = 1.4426950408889634
AXES = ("xh", "y", "xl", "z", "c")
XH, Y, XL, Z, C = 2, 4, 2, 8, 2
WIDE, SLIM, PACK, TERMS = 256, 128, 192, 16
f32, bf16 = jnp.float32, jnp.bfloat16


def trade(x):
    return lax.ppermute(x, ("xh", "c"), [(0, 0), (1, 2), (2, 1), (3, 3)])


def other_core(x):
    return lax.ppermute(x, "c", [(0, 1), (1, 0)])


def from_y(x, k):
    return lax.ppermute(x, "y", [(i, (i + k) % Y) for i in range(Y)])


def gather(own):
    return own, from_y(own, 1), from_y(own, -1), from_y(own, 2)


def dot(a, b):
    return lax.dot_general(a, b, (((1,), (0,)), ((), ())), preferred_element_type=f32)


def dot_cols(a, b):
    return lax.dot_general(a, b, (((1,), (1,)), ((), ())), preferred_element_type=f32)


def image_start(y):
    return pl.multiple_of(y * WIDE + jnp.where(y > 0, SLIM, 0), SLIM)


def text_start(y):
    return pl.multiple_of(y * WIDE, WIDE)


def join(parts, whole):
    at = 0
    for part in parts:
        whole[at : at + part.shape[0], :] = part[...]
        at += part.shape[0]


def finish(pre, square, emb, window, inv, unit, start, extra):
    inverse = lax.rsqrt(square + epsilon)
    value = pre * inverse
    unit[...] = value
    emb[...] = value.astype(bf16)
    inv[...] = jnp.broadcast_to(inverse, inv.shape)
    window[:, :WIDE] = unit[:, pl.ds(start, WIDE)]
    window[:, WIDE:] = unit[:, extra : extra + SLIM]


def text_kernel(ids, *refs):
    *pieces, weight, turned, emb, window, inv, joined, unit, held, arrived = refs
    copy = pltpu.make_async_copy(weight, held, arrived)
    copy.start()
    join(pieces, joined)
    features = joined[...]
    turned[...] = features.T
    copy.wait()
    pre = dot(features, held[...])
    square = jnp.sum(pre * pre, axis=1, keepdims=True)
    finish(pre, square, emb, window, inv, unit, text_start(ids[0]), weight.shape[1] - SLIM)


def image_kernel(ids, *refs):
    *pieces, weight, turned, emb, window, inv, joined, unit = refs
    join(pieces, joined)
    features = joined[...]
    pre = dot(features, weight[...])
    square = jnp.sum(pre * pre, axis=1, keepdims=True)
    finish(pre, square, emb, window, inv, unit, image_start(ids[0]), WIDE)
    turned[...] = features.T


def fold(x, combine):
    while x.shape[0] > 8:
        half = x.shape[0] // 2
        x = combine(x[:half], x[half:])
    return x


def stack(refs):
    return jnp.concatenate([ref[...] for ref in refs], axis=0)


def slope_kernel(
    ids, scal, p2, p3, weight, early, own, other,
    emb, turned, window, inv, slopes, slopes_turned, radial, text_radial, give, loss,
    late, joined, unit,
):
    y = ids[0]
    scale, bias = scal[0], scal[1]
    image_kernel(ids, p2, p3, weight, turned, late, window, inv, joined, unit)
    rows = emb.shape[0]
    join((early, late), emb)
    embedded = emb[...]
    lost = jnp.zeros((8, WIDE), f32)
    along = [jnp.zeros((WIDE, WIDE), f32) for _ in range(0, rows, WIDE)]
    scale2, bias2 = scale * LOG2_E, bias * LOG2_E
    for j in reversed(range(0, 2 * rows, WIDE)):
        mine = j < rows
        side, at = (own, j) if mine else (other, j - rows)
        cosines = dot_cols(embedded, side[at : at + WIDE, :])
        down = jnp.zeros((8, WIDE), f32)
        for i in range(0, rows, WIDE):
            cosine = cosines[i : i + WIDE]
            power = scale2 * cosine + bias2
            diagonal = mine and i == at
            if diagonal:
                same = lax.broadcasted_iota(jnp.int32, power.shape, 0) == lax.broadcasted_iota(
                    jnp.int32, power.shape, 1
                )
                power = jnp.where(same, -power, power)
            grown = jnp.exp2(power)
            whole = 1.0 + grown
            slope = grown * pl.reciprocal(whole, approx=True)
            if diagonal:
                slope = jnp.where(same, -slope, slope)
            lost = lost + fold(jnp.log(whole[: WIDE // 2] * whole[WIDE // 2 :]), jnp.add)
            slope = slope.astype(bf16)
            slopes[i : i + WIDE, j : j + WIDE] = slope
            slopes_turned[j : j + WIDE, i : i + WIDE] = slope.T
            weighted = slope.astype(f32) * cosine
            along[i // WIDE] = along[i // WIDE] + weighted
            down = down + fold(weighted, jnp.add)
        down = jnp.sum(down, axis=0, keepdims=True)
        down = jnp.transpose(jnp.broadcast_to(down, (SLIM, WIDE)))
        if mine:
            text_radial[at : at + WIDE, :] = down
        else:
            give[at : at + WIDE, WIDE + SLIM :] = down
    for i, part in enumerate(along):
        part = jnp.sum(part, axis=1, keepdims=True)
        radial[i * WIDE : (i + 1) * WIDE, :] = jnp.broadcast_to(part, (WIDE, SLIM))
    loss[...] = jnp.broadcast_to(jnp.sum(lost, keepdims=True), loss.shape)
    give[:, :WIDE] = dot(slopes_turned[rows:, :], emb[:, pl.ds(text_start(y), WIDE)])

    @pl.when(y == Y - 1)
    def _():
        give[:, WIDE : WIDE + SLIM] = dot(slopes_turned[rows:, :], emb[:, emb.shape[1] - SLIM :])

    @pl.when(y != Y - 1)
    def _():
        give[:, WIDE : WIDE + SLIM] = jnp.zeros((rows, SLIM), f32)


def wide(x, n):
    return jnp.concatenate([x] * (n // x.shape[1]), axis=1)


def back(grad, window, radial, inv):
    n = grad.shape[1]
    return ((grad - window * wide(radial, n)) * wide(inv, n)).astype(bf16)


def outer(turned, grad):
    return dot(jnp.concatenate([part[...] for part in turned], axis=1), grad)


def grad_kernel(
    ids, scal, f0, f1, w0, w1, v0, v1, emb, slopes, slopes_turned, radial, loss, own, other,
    term, part, rest,
):
    y = ids[0]
    scale = scal[0]
    rows = emb.shape[0]
    window, inv = stack((w0, w1)), stack((v0, v1))

    def columns(cols, at, size):
        grad = scale * (dot(slopes[:, :rows], own[:, cols]) + dot(slopes[:, rows:], other[:, cols]))
        grad = back(grad, window[:, at : at + size], scale * radial[...], inv)
        term[:, at : at + size] = outer((f0, f1), grad)

    n = rest.shape[0] - 8
    rest[:n, :] = dot(slopes_turned[rows : rows + n, :], emb[...])
    rest[n:, :] = jnp.broadcast_to(loss[:, :1], (8, rest.shape[1]))
    part[:, :WIDE] = dot(slopes_turned[:rows, :], emb[:, pl.ds(text_start(y), WIDE)])

    @pl.when(y == 0)
    def _():
        columns(slice(0, WIDE + SLIM), 0, WIDE + SLIM)

    @pl.when(y != 0)
    def _():
        columns(pl.ds(image_start(y), WIDE), 0, WIDE)

    @pl.when(y == Y - 1)
    def _():
        part[:, WIDE:] = dot(slopes_turned[:rows, :], emb[:, emb.shape[1] - SLIM :])

    @pl.when(y != Y - 1)
    def _():
        part[:, WIDE:] = jnp.zeros((rows, SLIM), f32)


def sum_kernel(
    ids, scal, turned, window, inv, text_radial, part, got, image_term,
    give, keep, token, term,
):
    y, c = ids[0], ids[1]
    scale = scal[0]
    grad = scale * (part[...] + got[:, : WIDE + SLIM])
    radial = scale * (text_radial[...] + got[:, WIDE + SLIM :])
    grad = back(grad, window[...], radial, inv[...])
    term[:, :WIDE] = dot(turned[...], grad[:, :WIDE])

    @pl.when(y == Y - 1)
    def _():
        term[:, WIDE:] = dot(turned[...], grad[:, WIDE:])

    @pl.when(y == 0)
    def _():
        term[:, WIDE:] = image_term[:, WIDE:]

    @pl.when((y != 0) & (y != Y - 1))
    def _():
        term[:, WIDE:] = jnp.zeros((term.shape[0], SLIM), f32)

    token[...] = jnp.zeros(token.shape, f32)
    for k in range(XL * Z):
        for core, out in ((c, keep), (1 - c, give)):
            packed = pack(image_term, term, k, core).astype(out.dtype)
            out[k] = packed


def pack(image_term, term, k, core):
    tiles = [(image_term, 0), (image_term, SLIM), (term, 0), (term, SLIM), (term, 2 * SLIM)]
    base = 72 * k
    whole = pl.ds(pl.multiple_of(base + 40 * core, 8), 32)
    parts = [source[whole, col : col + SLIM] for source, col in tiles]
    split = [source[base + 32 : base + 40, col : col + SLIM] for source, col in tiles]
    owned = lax.broadcasted_iota(jnp.int32, (8, SLIM), 0) // 4 == core
    parts += [jnp.where(owned, split[i], pltpu.roll(split[i + 1], 4, 0)) for i in (0, 2)]
    parts += [split[4], jnp.zeros((8, SLIM), f32)]
    return jnp.concatenate(parts, axis=0)


def add_kernel(keep, got, after, mine):
    del after
    mine[...] = (keep[...] + got[...].astype(f32)).astype(bf16)


def spread_kernel(parts, after, spread):
    del after
    summed = jnp.sum(parts[...].astype(f32), axis=0).astype(bf16)
    for i in range(spread.shape[0]):
        spread[i] = summed


def unpack_kernel(ids, spread, outs, image_out, text_out, loss, image_emb_out, text_emb_out):
    core = ids[1]
    n = image_emb_out.shape[1]
    image_emb_out[0] = outs[:n, :]
    text_emb_out[0] = outs[n : 2 * n, :]
    loss[0] = jnp.sum(outs[2 * n :, :SLIM].astype(f32)[:, :1])

    def place(c):
        for y in range(Y):
            rows = spread[y].astype(f32) + spread[Y + y].astype(f32)
            for tile in range(5):
                if tile < 2:
                    out, col = image_out, 2 * y + tile + (1 if y > 0 else 0)
                elif tile < 4:
                    out, col = text_out, 2 * y + tile - 2
                elif y == 0:
                    out, col = image_out, 2
                elif y == Y - 1:
                    out, col = text_out, 2 * Y
                else:
                    continue
                cols = slice(col * SLIM, (col + 1) * SLIM)
                shared = 160 + 8 * (tile // 2) + 4 * (c if tile % 2 == 0 else 1 - c)
                out[4 * c : 4 * c + 32, cols] = rows[32 * tile : 32 * tile + 32]
                out[32 * (1 - c) : 32 * (1 - c) + 4, cols] = rows[shared : shared + 4]

    for c in range(C):
        pl.when(core == c)(lambda c=c: place(c))


def out_kernel(scal, slopes, slopes_turned, emb, own, other, loss, got, after, out):
    del after
    scale = scal[0]
    n = got.shape[0] - 8
    rows = emb.shape[0]
    out[:n, :] = (scale * (dot(slopes[:n, :rows], own[...]) + dot(slopes[:n, rows:], other[...]))).astype(bf16)
    out[n : 2 * n, :] = (scale * (dot(slopes_turned[:n, :], emb[...]) + got[:n, :])).astype(bf16)
    left = (loss[:1, :1] + got[n : n + 1, :1]) * (1.0 / (C * rows))
    row = lax.broadcasted_iota(jnp.int32, (TERMS, out.shape[1]), 0)
    terms = jnp.zeros(row.shape, f32)
    for i in range(3):
        term = left.astype(bf16).astype(f32)
        terms = jnp.where(row == i, term, terms)
        left = left - term
    out[2 * n :, :] = terms.astype(bf16)


def call(kernel, outs, scratch=(), macs=0, far=None):
    def space(i, x):
        if i == far:
            return pltpu.HBM
        return pltpu.SMEM if x.ndim == 1 else pltpu.VMEM

    def run(*args):
        return pl.pallas_call(
            kernel,
            out_shape=[jax.ShapeDtypeStruct(s, d) for s, d in outs],
            in_specs=[pl.BlockSpec(memory_space=space(i, a)) for i, a in enumerate(args)],
            out_specs=[pl.BlockSpec(memory_space=pltpu.SMEM if len(s) == 1 else pltpu.VMEM) for s, _ in outs],
            scratch_shapes=list(scratch),
            compiler_params=pltpu.CompilerParams(vmem_limit_bytes=16 * 2**20),
            cost_estimate=pl.CostEstimate(flops=2 * macs, bytes_accessed=0, transcendentals=0),
        )(*args)

    return run


def on_device(image_feats, text_feats, image_proj, text_proj, logit_scale, logit_bias):
    c, y = lax.axis_index("c"), lax.axis_index("y")
    ids = jnp.stack([y, c]).astype(jnp.int32)
    scal = jnp.concatenate([logit_scale, logit_bias])
    n, depth = image_feats.shape[1:]
    width = image_proj.shape[1]
    rows = n * Y
    macs = 20 * rows * depth * width

    def projected(count):
        return [((depth, count), bf16), ((count, width), bf16), ((count, WIDE + SLIM), f32), ((count, SLIM), f32)]

    def scratch(count):
        return [pltpu.VMEM((count, depth), bf16), pltpu.VMEM((count, width), f32)]

    text = gather(trade(text_feats[0]))
    image = gather(trade(image_feats[0]))
    streams = [pltpu.VMEM((depth, width), bf16), pltpu.SemaphoreType.DMA]
    text_turned, text_emb, text_window, text_inv = call(
        text_kernel, projected(rows), scratch(rows) + streams, macs, len(text) + 1
    )(ids, *text, pltpu.with_memory_space_constraint(text_proj, pltpu.HBM))
    text_other = other_core(text_emb)
    turned_a, early, window_a, inv_a = call(image_kernel, projected(2 * n), scratch(2 * n), macs)(
        ids, *image[:2], image_proj
    )
    turned, _, window, inv = projected(2 * n)
    emb, turned_b, window_b, inv_b, slopes, slopes_turned, radial, text_radial, give, loss = call(
        slope_kernel,
        [
            ((rows, width), bf16), turned, window, inv,
            ((rows, C * rows), bf16), ((C * rows, rows), bf16), ((rows, SLIM), f32), ((rows, SLIM), f32),
            ((rows, WIDE + 2 * SLIM), f32), ((8, SLIM), f32),
        ],
        [pltpu.VMEM((2 * n, width), bf16)] + scratch(2 * n),
        macs,
    )(ids, scal, *image[2:], image_proj, early, text_emb, text_other)
    got = other_core(give)
    image_term, part, rest = call(
        grad_kernel, [((depth, WIDE + SLIM), f32), ((rows, WIDE + SLIM), f32), ((n + 8, width), f32)], (), macs
    )(
        ids, scal, turned_a, turned_b, window_a, window_b, inv_a, inv_b, emb, slopes, slopes_turned,
        radial, loss, text_emb, text_other,
    )
    packed = (XL * Z, PACK, SLIM)
    give, keep, token = call(
        sum_kernel,
        [(packed, bf16), (packed, f32), ((8, SLIM), f32)],
        [pltpu.VMEM((depth, WIDE + SLIM), f32)],
    )(ids, scal, text_turned, text_window, text_inv, text_radial, part, got, image_term)
    (outs,) = call(out_kernel, [((2 * n + TERMS, width), bf16)], (), macs)(
        scal, slopes, slopes_turned, emb, text_emb, text_other, loss, other_core(rest), token
    )
    (mine,) = call(add_kernel, [(packed, bf16)])(keep, other_core(give), outs)
    outs = trade(outs)
    arrived = lax.all_to_all(mine, ("xl", "z"), 0, 0)
    (spread,) = call(spread_kernel, [((XH * Y, PACK, SLIM), bf16)])(arrived, outs)
    spread = lax.all_to_all(spread, ("xh", "y"), 0, 0)
    grad = (depth // (XL * Z * C), width), f32
    image_grad, text_grad, total, image_out, text_out = call(
        unpack_kernel, [grad, grad, ((1,), f32), ((1, n, width), bf16), ((1, n, width), bf16)]
    )(ids, spread, outs)
    return total, image_grad, text_grad, image_out, text_out


def solution(mesh):
    fine = Mesh(mesh.devices.reshape(XH, Y, XL, Z, C), AXES)
    dp, blk = ("xl", "z", "c"), ("xh", "y")
    in_specs = (P(dp, blk, None), P(dp, blk, None), P(), P(), P(), P())
    out_specs = (P(dp), P(dp, None), P(dp, None), P(dp, blk, None), P(dp, blk, None))
    return jax.shard_map(
        on_device, mesh=fine, in_specs=in_specs, out_specs=out_specs, check_vma=False
    )
```

```python
import jax
import jax.numpy as jnp
from jax import lax
from jax.experimental import pallas as pl
from jax.experimental.pallas import tpu as pltpu
from jax.sharding import Mesh, PartitionSpec as P

epsilon = 1e-06
LOG2_E = 1.4426950408889634
AXES = ("xh", "y", "xl", "z", "c")
XH, Y, XL, Z, C = 2, 4, 2, 8, 2
WIDE, SLIM, PACK, TERMS = 256, 128, 184, 16
f32, bf16 = jnp.float32, jnp.bfloat16


def trade(x):
    return lax.ppermute(x, ("xh", "c"), [(0, 0), (1, 2), (2, 1), (3, 3)])


def other_core(x):
    return lax.ppermute(x, "c", [(0, 1), (1, 0)])


def from_y(x, k):
    return lax.ppermute(x, "y", [(i, (i + k) % Y) for i in range(Y)])


def gather(own):
    return own, from_y(own, 1), from_y(own, -1), from_y(own, 2)


def dot(a, b):
    return lax.dot_general(a, b, (((1,), (0,)), ((), ())), preferred_element_type=f32)


def dot_cols(a, b):
    return lax.dot_general(a, b, (((1,), (1,)), ((), ())), preferred_element_type=f32)


def image_start(y):
    return pl.multiple_of(y * WIDE + jnp.where(y > 0, SLIM, 0), SLIM)


def text_start(y):
    return pl.multiple_of(y * WIDE, WIDE)


def join(parts, whole):
    at = 0
    for part in parts:
        whole[at : at + part.shape[0], :] = part[...]
        at += part.shape[0]


def finish(pre, square, emb, window, inv, unit, start, extra):
    inverse = lax.rsqrt(square + epsilon)
    value = pre * inverse
    unit[...] = value
    emb[...] = value.astype(bf16)
    inv[...] = jnp.broadcast_to(inverse, inv.shape)
    window[:, :WIDE] = unit[:, pl.ds(start, WIDE)]
    window[:, WIDE:] = unit[:, extra : extra + SLIM]


def text_kernel(ids, *refs):
    *pieces, weight, turned, emb, window, inv, joined, unit, held, arrived = refs
    copy = pltpu.make_async_copy(weight, held, arrived)
    copy.start()
    join(pieces, joined)
    features = joined[...]
    turned[...] = features.T
    copy.wait()
    pre = dot(features, held[...])
    square = jnp.sum(pre * pre, axis=1, keepdims=True)
    finish(pre, square, emb, window, inv, unit, text_start(ids[0]), weight.shape[1] - SLIM)


def image_kernel(ids, *refs):
    *pieces, weight, turned, emb, window, inv, joined, unit = refs
    join(pieces, joined)
    features = joined[...]
    pre = dot(features, weight[...])
    square = jnp.sum(pre * pre, axis=1, keepdims=True)
    finish(pre, square, emb, window, inv, unit, image_start(ids[0]), WIDE)
    turned[...] = features.T


def fold(x, combine):
    while x.shape[0] > 8:
        half = x.shape[0] // 2
        x = combine(x[:half], x[half:])
    return x


def stack(refs):
    return jnp.concatenate([ref[...] for ref in refs], axis=0)


def slope_kernel(
    ids, scal, p2, p3, weight, early, own, other,
    emb, turned, window, inv, slopes, slopes_turned, radial, text_radial, give, loss,
    late, joined, unit,
):
    y = ids[0]
    scale, bias = scal[0], scal[1]
    image_kernel(ids, p2, p3, weight, turned, late, window, inv, joined, unit)
    rows = emb.shape[0]
    join((early, late), emb)
    embedded = emb[...]
    lost = jnp.zeros((8, WIDE), f32)
    along = [jnp.zeros((WIDE, WIDE), f32) for _ in range(0, rows, WIDE)]
    scale2, bias2 = scale * LOG2_E, bias * LOG2_E
    for j in reversed(range(0, 2 * rows, WIDE)):
        mine = j < rows
        side, at = (own, j) if mine else (other, j - rows)
        cosines = dot_cols(embedded, side[at : at + WIDE, :])
        down = jnp.zeros((8, WIDE), f32)
        for i in range(0, rows, WIDE):
            cosine = cosines[i : i + WIDE]
            power = scale2 * cosine + bias2
            diagonal = mine and i == at
            if diagonal:
                same = lax.broadcasted_iota(jnp.int32, power.shape, 0) == lax.broadcasted_iota(
                    jnp.int32, power.shape, 1
                )
                power = jnp.where(same, -power, power)
            grown = jnp.exp2(power)
            whole = 1.0 + grown
            slope = grown * pl.reciprocal(whole, approx=True)
            if diagonal:
                slope = jnp.where(same, -slope, slope)
            lost = lost + fold(jnp.log(whole[: WIDE // 2] * whole[WIDE // 2 :]), jnp.add)
            slope = slope.astype(bf16)
            slopes[i : i + WIDE, j : j + WIDE] = slope
            slopes_turned[j : j + WIDE, i : i + WIDE] = slope.T
            weighted = slope.astype(f32) * cosine
            along[i // WIDE] = along[i // WIDE] + weighted
            down = down + fold(weighted, jnp.add)
        down = jnp.sum(down, axis=0, keepdims=True)
        down = jnp.transpose(jnp.broadcast_to(down, (SLIM, WIDE)))
        if mine:
            text_radial[at : at + WIDE, :] = down
        else:
            give[at : at + WIDE, WIDE + SLIM :] = down
    for i, part in enumerate(along):
        part = jnp.sum(part, axis=1, keepdims=True)
        radial[i * WIDE : (i + 1) * WIDE, :] = jnp.broadcast_to(part, (WIDE, SLIM))
    loss[...] = jnp.broadcast_to(jnp.sum(lost, keepdims=True), loss.shape)
    give[:, :WIDE] = dot(slopes_turned[rows:, :], emb[:, pl.ds(text_start(y), WIDE)])

    @pl.when(y == Y - 1)
    def _():
        give[:, WIDE : WIDE + SLIM] = dot(slopes_turned[rows:, :], emb[:, emb.shape[1] - SLIM :])

    @pl.when(y != Y - 1)
    def _():
        give[:, WIDE : WIDE + SLIM] = jnp.zeros((rows, SLIM), f32)


def wide(x, n):
    return jnp.concatenate([x] * (n // x.shape[1]), axis=1)


def back(grad, window, radial, inv):
    n = grad.shape[1]
    return ((grad - window * wide(radial, n)) * wide(inv, n)).astype(bf16)


def outer(turned, grad):
    return dot(jnp.concatenate([part[...] for part in turned], axis=1), grad)


def grad_kernel(
    ids, scal, f0, f1, w0, w1, v0, v1, emb, slopes, slopes_turned, radial, loss, own, other,
    term, part, rest,
):
    y = ids[0]
    scale = scal[0]
    rows = emb.shape[0]
    window, inv = stack((w0, w1)), stack((v0, v1))

    def columns(cols, at, size):
        grad = scale * (dot(slopes[:, :rows], own[:, cols]) + dot(slopes[:, rows:], other[:, cols]))
        grad = back(grad, window[:, at : at + size], scale * radial[...], inv)
        term[:, at : at + size] = outer((f0, f1), grad)

    n = rest.shape[0] - 8
    rest[:n, :] = dot(slopes_turned[rows : rows + n, :], emb[...])
    rest[n:, :] = jnp.broadcast_to(loss[:, :1], (8, rest.shape[1]))
    part[:, :WIDE] = dot(slopes_turned[:rows, :], emb[:, pl.ds(text_start(y), WIDE)])

    @pl.when(y == 0)
    def _():
        columns(slice(0, WIDE + SLIM), 0, WIDE + SLIM)

    @pl.when(y != 0)
    def _():
        columns(pl.ds(image_start(y), WIDE), 0, WIDE)

    @pl.when(y == Y - 1)
    def _():
        part[:, WIDE:] = dot(slopes_turned[:rows, :], emb[:, emb.shape[1] - SLIM :])

    @pl.when(y != Y - 1)
    def _():
        part[:, WIDE:] = jnp.zeros((rows, SLIM), f32)


def sum_kernel(
    ids, scal, turned, window, inv, text_radial, part, got, image_term,
    give, keep, token, term,
):
    y, c = ids[0], ids[1]
    scale = scal[0]
    grad = scale * (part[...] + got[:, : WIDE + SLIM])
    radial = scale * (text_radial[...] + got[:, WIDE + SLIM :])
    grad = back(grad, window[...], radial, inv[...])
    term[:, :WIDE] = dot(turned[...], grad[:, :WIDE])

    @pl.when(y == Y - 1)
    def _():
        term[:, WIDE:] = dot(turned[...], grad[:, WIDE:])

    @pl.when(y == 0)
    def _():
        term[:, WIDE:] = image_term[:, WIDE:]

    @pl.when((y != 0) & (y != Y - 1))
    def _():
        term[:, WIDE:] = jnp.zeros((term.shape[0], SLIM), f32)

    token[...] = jnp.zeros(token.shape, f32)
    for k in range(XL * Z):
        for core, out in ((c, keep), (1 - c, give)):
            packed = pack(image_term, term, k, core).astype(out.dtype)
            out[k] = packed


def pack(image_term, term, k, core):
    tiles = [(image_term, 0), (image_term, SLIM), (term, 0), (term, SLIM), (term, 2 * SLIM)]
    base = 72 * k
    whole = pl.ds(pl.multiple_of(base + 40 * core, 8), 32)
    parts = [source[whole, col : col + SLIM] for source, col in tiles]
    split = [source[base + 32 : base + 40, col : col + SLIM] for source, col in tiles]
    owned = lax.broadcasted_iota(jnp.int32, (8, SLIM), 0) // 4 == core
    parts += [jnp.where(owned, split[i], pltpu.roll(split[i + 1], 4, 0)) for i in (0, 2)]
    parts.append(split[4])
    return jnp.concatenate(parts, axis=0)


def add_kernel(keep, got, after, mine, held, sent):
    del after
    step = held.shape[0] // sent.shape[0]
    copies = []
    for i in range(sent.shape[0]):
        part = pl.ds(i * step, step)
        held[part] = (keep[part] + got[part].astype(f32)).astype(bf16)
        copies.append(pltpu.make_async_copy(held.at[part], mine.at[part], sent.at[i]))
        copies[-1].start()
    for copy in copies:
        copy.wait()


def spread_kernel(parts, after, spread):
    del after
    summed = jnp.sum(parts[...].astype(f32), axis=0).astype(bf16)
    for i in range(spread.shape[0]):
        spread[i] = summed


def unpack_kernel(ids, spread, outs, image_out, text_out, loss, image_emb_out, text_emb_out):
    core = ids[1]
    n = image_emb_out.shape[1]
    image_emb_out[0] = outs[:n, :]
    text_emb_out[0] = outs[n : 2 * n, :]
    loss[0] = jnp.sum(outs[2 * n :, :SLIM].astype(f32)[:, :1])

    def place(c):
        for y in range(Y):
            rows = spread[y].astype(f32) + spread[Y + y].astype(f32)
            for tile in range(5):
                if tile < 2:
                    out, col = image_out, 2 * y + tile + (1 if y > 0 else 0)
                elif tile < 4:
                    out, col = text_out, 2 * y + tile - 2
                elif y == 0:
                    out, col = image_out, 2
                elif y == Y - 1:
                    out, col = text_out, 2 * Y
                else:
                    continue
                cols = slice(col * SLIM, (col + 1) * SLIM)
                shared = 160 + 8 * (tile // 2) + 4 * (c if tile % 2 == 0 else 1 - c)
                out[4 * c : 4 * c + 32, cols] = rows[32 * tile : 32 * tile + 32]
                out[32 * (1 - c) : 32 * (1 - c) + 4, cols] = rows[shared : shared + 4]

    for c in range(C):
        pl.when(core == c)(lambda c=c: place(c))


def out_kernel(scal, slopes, slopes_turned, emb, own, other, loss, got, after, out):
    del after
    scale = scal[0]
    n = got.shape[0] - 8
    rows = emb.shape[0]
    out[:n, :] = (scale * (dot(slopes[:n, :rows], own[...]) + dot(slopes[:n, rows:], other[...]))).astype(bf16)
    out[n : 2 * n, :] = (scale * (dot(slopes_turned[:n, :], emb[...]) + got[:n, :])).astype(bf16)
    left = (loss[:1, :1] + got[n : n + 1, :1]) * (1.0 / (C * rows))
    row = lax.broadcasted_iota(jnp.int32, (TERMS, out.shape[1]), 0)
    terms = jnp.zeros(row.shape, f32)
    for i in range(3):
        term = left.astype(bf16).astype(f32)
        terms = jnp.where(row == i, term, terms)
        left = left - term
    out[2 * n :, :] = terms.astype(bf16)


def call(kernel, outs, scratch=(), macs=0, far=None, result=pltpu.VMEM):
    def space(i, x):
        if i == far:
            return pltpu.HBM
        return pltpu.SMEM if x.ndim == 1 else pltpu.VMEM

    def run(*args):
        return pl.pallas_call(
            kernel,
            out_shape=[jax.ShapeDtypeStruct(s, d) for s, d in outs],
            in_specs=[pl.BlockSpec(memory_space=space(i, a)) for i, a in enumerate(args)],
            out_specs=[pl.BlockSpec(memory_space=pltpu.SMEM if len(s) == 1 else result) for s, _ in outs],
            scratch_shapes=list(scratch),
            compiler_params=pltpu.CompilerParams(vmem_limit_bytes=16 * 2**20),
            cost_estimate=pl.CostEstimate(flops=2 * macs, bytes_accessed=0, transcendentals=0),
        )(*args)

    return run


def on_device(image_feats, text_feats, image_proj, text_proj, logit_scale, logit_bias):
    c, y = lax.axis_index("c"), lax.axis_index("y")
    ids = jnp.stack([y, c]).astype(jnp.int32)
    scal = jnp.concatenate([logit_scale, logit_bias])
    n, depth = image_feats.shape[1:]
    width = image_proj.shape[1]
    rows = n * Y
    macs = 20 * rows * depth * width

    def projected(count):
        return [((depth, count), bf16), ((count, width), bf16), ((count, WIDE + SLIM), f32), ((count, SLIM), f32)]

    def scratch(count):
        return [pltpu.VMEM((count, depth), bf16), pltpu.VMEM((count, width), f32)]

    text = gather(trade(text_feats[0]))
    image = gather(trade(image_feats[0]))
    streams = [pltpu.VMEM((depth, width), bf16), pltpu.SemaphoreType.DMA]
    text_turned, text_emb, text_window, text_inv = call(
        text_kernel, projected(rows), scratch(rows) + streams, macs, len(text) + 1
    )(ids, *text, pltpu.with_memory_space_constraint(text_proj, pltpu.HBM))
    text_other = other_core(text_emb)
    turned_a, early, window_a, inv_a = call(image_kernel, projected(2 * n), scratch(2 * n), macs)(
        ids, *image[:2], image_proj
    )
    turned, _, window, inv = projected(2 * n)
    emb, turned_b, window_b, inv_b, slopes, slopes_turned, radial, text_radial, give, loss = call(
        slope_kernel,
        [
            ((rows, width), bf16), turned, window, inv,
            ((rows, C * rows), bf16), ((C * rows, rows), bf16), ((rows, SLIM), f32), ((rows, SLIM), f32),
            ((rows, WIDE + 2 * SLIM), f32), ((8, SLIM), f32),
        ],
        [pltpu.VMEM((2 * n, width), bf16)] + scratch(2 * n),
        macs,
    )(ids, scal, *image[2:], image_proj, early, text_emb, text_other)
    got = other_core(give)
    image_term, part, rest = call(
        grad_kernel, [((depth, WIDE + SLIM), f32), ((rows, WIDE + SLIM), f32), ((n + 8, width), f32)], (), macs
    )(
        ids, scal, turned_a, turned_b, window_a, window_b, inv_a, inv_b, emb, slopes, slopes_turned,
        radial, loss, text_emb, text_other,
    )
    packed = (XL * Z, PACK, SLIM)
    give, keep, token = call(
        sum_kernel,
        [(packed, bf16), (packed, f32), ((8, SLIM), f32)],
        [pltpu.VMEM((depth, WIDE + SLIM), f32)],
    )(ids, scal, text_turned, text_window, text_inv, text_radial, part, got, image_term)
    (outs,) = call(out_kernel, [((2 * n + TERMS, width), bf16)], (), macs)(
        scal, slopes, slopes_turned, emb, text_emb, text_other, loss, other_core(rest), token
    )
    (mine,) = call(
        add_kernel, [(packed, bf16)], [pltpu.VMEM(packed, bf16), pltpu.SemaphoreType.DMA((4,))], 0, None, pl.ANY
    )(keep, other_core(give), outs)
    outs = trade(outs)
    arrived = lax.all_to_all(mine, ("xl", "z"), 0, 0)
    (spread,) = call(spread_kernel, [((XH * Y, PACK, SLIM), bf16)])(arrived, outs)
    spread = lax.all_to_all(spread, ("xh", "y"), 0, 0)
    grad = (depth // (XL * Z * C), width), f32
    image_grad, text_grad, total, image_out, text_out = call(
        unpack_kernel, [grad, grad, ((1,), f32), ((1, n, width), bf16), ((1, n, width), bf16)]
    )(ids, spread, outs)
    return total, image_grad, text_grad, image_out, text_out


def solution(mesh):
    fine = Mesh(mesh.devices.reshape(XH, Y, XL, Z, C), AXES)
    dp, blk = ("xl", "z", "c"), ("xh", "y")
    in_specs = (P(dp, blk, None), P(dp, blk, None), P(), P(), P(), P())
    out_specs = (P(dp), P(dp, None), P(dp, None), P(dp, blk, None), P(dp, blk, None))
    return jax.shard_map(
        on_device, mesh=fine, in_specs=in_specs, out_specs=out_specs, check_vma=False
    )
```

```python
import jax
import jax.numpy as jnp
from jax import lax
from jax.experimental import pallas as pl
from jax.experimental.pallas import tpu as pltpu
from jax.sharding import Mesh, PartitionSpec as P

epsilon = 1e-06
LOG2_E = 1.4426950408889634
AXES = ("xh", "y", "xl", "z", "c")
XH, Y, XL, Z, C = 2, 4, 2, 8, 2
WIDE, SLIM, PACK, TERMS = 256, 128, 184, 16
f32, bf16 = jnp.float32, jnp.bfloat16


def trade(x):
    return lax.ppermute(x, ("xh", "c"), [(0, 0), (1, 2), (2, 1), (3, 3)])


def other_core(x):
    return lax.ppermute(x, "c", [(0, 1), (1, 0)])


def from_y(x, k):
    return lax.ppermute(x, "y", [(i, (i + k) % Y) for i in range(Y)])


def gather(own):
    return own, from_y(own, 1), from_y(own, -1), from_y(own, 2)


def dot(a, b):
    return lax.dot_general(a, b, (((1,), (0,)), ((), ())), preferred_element_type=f32)


def dot_cols(a, b):
    return lax.dot_general(a, b, (((1,), (1,)), ((), ())), preferred_element_type=f32)


def image_start(y):
    return pl.multiple_of(y * WIDE + jnp.where(y > 0, SLIM, 0), SLIM)


def text_start(y):
    return pl.multiple_of(y * WIDE, WIDE)


def join(parts, whole):
    at = 0
    for part in parts:
        whole[at : at + part.shape[0], :] = part[...]
        at += part.shape[0]


def finish(pre, square, emb, window, inv, unit, start, extra):
    inverse = lax.rsqrt(square + epsilon)
    value = pre * inverse
    unit[...] = value
    emb[...] = value.astype(bf16)
    inv[...] = jnp.broadcast_to(inverse, inv.shape)
    window[:, :WIDE] = unit[:, pl.ds(start, WIDE)]
    window[:, WIDE:] = unit[:, extra : extra + SLIM]


def text_kernel(ids, *refs):
    *pieces, weight, turned, emb, window, inv, joined, unit, held, arrived = refs
    copy = pltpu.make_async_copy(weight, held, arrived)
    copy.start()
    join(pieces, joined)
    features = joined[...]
    turned[...] = features.T
    copy.wait()
    pre = dot(features, held[...])
    square = jnp.sum(pre * pre, axis=1, keepdims=True)
    finish(pre, square, emb, window, inv, unit, text_start(ids[0]), weight.shape[1] - SLIM)


def image_kernel(ids, *refs):
    *pieces, weight, turned, emb, window, inv, joined, unit = refs
    join(pieces, joined)
    features = joined[...]
    pre = dot(features, weight[...])
    square = jnp.sum(pre * pre, axis=1, keepdims=True)
    finish(pre, square, emb, window, inv, unit, image_start(ids[0]), WIDE)
    turned[...] = features.T


def fold(x, combine):
    while x.shape[0] > 8:
        half = x.shape[0] // 2
        x = combine(x[:half], x[half:])
    return x


def stack(refs):
    return jnp.concatenate([ref[...] for ref in refs], axis=0)


def slope_kernel(
    ids, scal, p2, p3, weight, early, own, other,
    emb, turned, window, inv, slopes, slopes_turned, radial, text_radial, give, loss,
    late, joined, unit,
):
    y = ids[0]
    scale, bias = scal[0], scal[1]
    image_kernel(ids, p2, p3, weight, turned, late, window, inv, joined, unit)
    rows = emb.shape[0]
    join((early, late), emb)
    embedded = emb[...]
    lost = jnp.zeros((8, WIDE), f32)
    along = [jnp.zeros((WIDE, WIDE), f32) for _ in range(0, rows, WIDE)]
    scale2, bias2 = scale * LOG2_E, bias * LOG2_E
    for j in reversed(range(0, 2 * rows, WIDE)):
        mine = j < rows
        side, at = (own, j) if mine else (other, j - rows)
        cosines = dot_cols(embedded, side[at : at + WIDE, :])
        down = jnp.zeros((8, WIDE), f32)
        for i in range(0, rows, WIDE):
            cosine = cosines[i : i + WIDE]
            power = scale2 * cosine + bias2
            diagonal = mine and i == at
            if diagonal:
                same = lax.broadcasted_iota(jnp.int32, power.shape, 0) == lax.broadcasted_iota(
                    jnp.int32, power.shape, 1
                )
                power = jnp.where(same, -power, power)
            grown = jnp.exp2(power)
            whole = 1.0 + grown
            slope = grown * pl.reciprocal(whole, approx=True)
            if diagonal:
                slope = jnp.where(same, -slope, slope)
            lost = lost + fold(jnp.log(whole[: WIDE // 2] * whole[WIDE // 2 :]), jnp.add)
            slope = slope.astype(bf16)
            slopes[i : i + WIDE, j : j + WIDE] = slope
            slopes_turned[j : j + WIDE, i : i + WIDE] = slope.T
            weighted = slope.astype(f32) * cosine
            along[i // WIDE] = along[i // WIDE] + weighted
            down = down + fold(weighted, jnp.add)
        down = jnp.sum(down, axis=0, keepdims=True)
        down = jnp.transpose(jnp.broadcast_to(down, (SLIM, WIDE)))
        if mine:
            text_radial[at : at + WIDE, :] = down
        else:
            give[at : at + WIDE, WIDE + SLIM :] = down
    for i, part in enumerate(along):
        part = jnp.sum(part, axis=1, keepdims=True)
        radial[i * WIDE : (i + 1) * WIDE, :] = jnp.broadcast_to(part, (WIDE, SLIM))
    loss[...] = jnp.broadcast_to(jnp.sum(lost, keepdims=True), loss.shape)
    give[:, :WIDE] = dot(slopes_turned[rows:, :], emb[:, pl.ds(text_start(y), WIDE)])

    @pl.when(y == Y - 1)
    def _():
        give[:, WIDE : WIDE + SLIM] = dot(slopes_turned[rows:, :], emb[:, emb.shape[1] - SLIM :])

    @pl.when(y != Y - 1)
    def _():
        give[:, WIDE : WIDE + SLIM] = jnp.zeros((rows, SLIM), f32)


def wide(x, n):
    return jnp.concatenate([x] * (n // x.shape[1]), axis=1)


def back(grad, window, radial, inv):
    n = grad.shape[1]
    return ((grad - window * wide(radial, n)) * wide(inv, n)).astype(bf16)


def outer(turned, grad):
    return dot(jnp.concatenate([part[...] for part in turned], axis=1), grad)


def grad_kernel(
    ids, scal, f0, f1, w0, w1, v0, v1, emb, slopes, slopes_turned, radial, loss, own, other,
    term, part, rest,
):
    y = ids[0]
    scale = scal[0]
    rows = emb.shape[0]
    window, inv = stack((w0, w1)), stack((v0, v1))

    def columns(cols, at, size):
        grad = scale * (dot(slopes[:, :rows], own[:, cols]) + dot(slopes[:, rows:], other[:, cols]))
        grad = back(grad, window[:, at : at + size], scale * radial[...], inv)
        term[:, at : at + size] = outer((f0, f1), grad)

    n = rest.shape[0] - 8
    rest[:n, :] = dot(slopes_turned[rows : rows + n, :], emb[...])
    rest[n:, :] = jnp.broadcast_to(loss[:, :1], (8, rest.shape[1]))

    @pl.when(y == 0)
    def _():
        columns(slice(0, WIDE + SLIM), 0, WIDE + SLIM)

    @pl.when(y != 0)
    def _():
        columns(pl.ds(image_start(y), WIDE), 0, WIDE)

    @pl.when(y == Y - 1)
    def _():
        part[...] = dot(slopes_turned[:rows, :], emb[:, emb.shape[1] - WIDE - SLIM :])

    @pl.when(y != Y - 1)
    def _():
        part[:, :WIDE] = dot(slopes_turned[:rows, :], emb[:, pl.ds(text_start(y), WIDE)])
        part[:, WIDE:] = jnp.zeros((rows, SLIM), f32)


def sum_kernel(
    ids, scal, turned, window, inv, text_radial, part, got, image_term,
    give, keep, token, term,
):
    y, c = ids[0], ids[1]
    scale = scal[0]
    grad = scale * (part[...] + got[:, : WIDE + SLIM])
    radial = scale * (text_radial[...] + got[:, WIDE + SLIM :])
    grad = back(grad, window[...], radial, inv[...])

    @pl.when(y == Y - 1)
    def _():
        term[...] = dot(turned[...], grad)

    @pl.when(y != Y - 1)
    def _():
        term[:, :WIDE] = dot(turned[...], grad[:, :WIDE])

    @pl.when(y == 0)
    def _():
        term[:, WIDE:] = image_term[:, WIDE:]

    @pl.when((y != 0) & (y != Y - 1))
    def _():
        term[:, WIDE:] = jnp.zeros((term.shape[0], SLIM), f32)

    token[...] = jnp.zeros(token.shape, f32)
    for k in range(XL * Z):
        for core, out in ((c, keep), (1 - c, give)):
            packed = pack(image_term, term, k, core).astype(out.dtype)
            out[k] = packed


def pack(image_term, term, k, core):
    tiles = [(image_term, 0), (image_term, SLIM), (term, 0), (term, SLIM), (term, 2 * SLIM)]
    base = 72 * k
    whole = pl.ds(pl.multiple_of(base + 40 * core, 8), 32)
    parts = [source[whole, col : col + SLIM] for source, col in tiles]
    split = [source[base + 32 : base + 40, col : col + SLIM] for source, col in tiles]
    owned = lax.broadcasted_iota(jnp.int32, (8, SLIM), 0) // 4 == core
    parts += [jnp.where(owned, split[i], pltpu.roll(split[i + 1], 4, 0)) for i in (0, 2)]
    parts.append(split[4])
    return jnp.concatenate(parts, axis=0)


def add_kernel(keep, got, after, mine, held, sent):
    del after
    step = held.shape[0] // sent.shape[0]
    copies = []
    for i in range(sent.shape[0]):
        part = pl.ds(i * step, step)
        held[part] = (keep[part] + got[part].astype(f32)).astype(bf16)
        copies.append(pltpu.make_async_copy(held.at[part], mine.at[part], sent.at[i]))
        copies[-1].start()
    for copy in copies:
        copy.wait()


def spread_kernel(parts, after, spread):
    del after
    summed = jnp.sum(parts[...].astype(f32), axis=0).astype(bf16)
    for i in range(spread.shape[0]):
        spread[i] = summed


def unpack_kernel(ids, spread, outs, image_out, text_out, loss, image_emb_out, text_emb_out):
    core = ids[1]
    n = image_emb_out.shape[1]
    image_emb_out[0] = outs[:n, :]
    text_emb_out[0] = outs[n : 2 * n, :]
    loss[0] = jnp.sum(outs[2 * n :, :SLIM].astype(f32)[:, :1])

    def place(c):
        for y in range(Y):
            rows = spread[y].astype(f32) + spread[Y + y].astype(f32)
            for tile in range(5):
                if tile < 2:
                    out, col = image_out, 2 * y + tile + (1 if y > 0 else 0)
                elif tile < 4:
                    out, col = text_out, 2 * y + tile - 2
                elif y == 0:
                    out, col = image_out, 2
                elif y == Y - 1:
                    out, col = text_out, 2 * Y
                else:
                    continue
                cols = slice(col * SLIM, (col + 1) * SLIM)
                shared = 160 + 8 * (tile // 2) + 4 * (c if tile % 2 == 0 else 1 - c)
                out[4 * c : 4 * c + 32, cols] = rows[32 * tile : 32 * tile + 32]
                out[32 * (1 - c) : 32 * (1 - c) + 4, cols] = rows[shared : shared + 4]

    for c in range(C):
        pl.when(core == c)(lambda c=c: place(c))


def out_kernel(scal, slopes, slopes_turned, emb, own, other, loss, got, after, out):
    del after
    scale = scal[0]
    n = got.shape[0] - 8
    rows = emb.shape[0]
    out[:n, :] = (scale * (dot(slopes[:n, :rows], own[...]) + dot(slopes[:n, rows:], other[...]))).astype(bf16)
    out[n : 2 * n, :] = (scale * (dot(slopes_turned[:n, :], emb[...]) + got[:n, :])).astype(bf16)
    left = (loss[:1, :1] + got[n : n + 1, :1]) * (1.0 / (C * rows))
    row = lax.broadcasted_iota(jnp.int32, (TERMS, out.shape[1]), 0)
    terms = jnp.zeros(row.shape, f32)
    for i in range(3):
        term = left.astype(bf16).astype(f32)
        terms = jnp.where(row == i, term, terms)
        left = left - term
    out[2 * n :, :] = terms.astype(bf16)


def call(kernel, outs, scratch=(), macs=0, far=None, result=pltpu.VMEM):
    def space(i, x):
        if i == far:
            return pltpu.HBM
        return pltpu.SMEM if x.ndim == 1 else pltpu.VMEM

    def run(*args):
        return pl.pallas_call(
            kernel,
            out_shape=[jax.ShapeDtypeStruct(s, d) for s, d in outs],
            in_specs=[pl.BlockSpec(memory_space=space(i, a)) for i, a in enumerate(args)],
            out_specs=[pl.BlockSpec(memory_space=pltpu.SMEM if len(s) == 1 else result) for s, _ in outs],
            scratch_shapes=list(scratch),
            compiler_params=pltpu.CompilerParams(vmem_limit_bytes=16 * 2**20),
            cost_estimate=pl.CostEstimate(flops=2 * macs, bytes_accessed=0, transcendentals=0),
        )(*args)

    return run


def on_device(image_feats, text_feats, image_proj, text_proj, logit_scale, logit_bias):
    c, y = lax.axis_index("c"), lax.axis_index("y")
    ids = jnp.stack([y, c]).astype(jnp.int32)
    scal = jnp.concatenate([logit_scale, logit_bias])
    n, depth = image_feats.shape[1:]
    width = image_proj.shape[1]
    rows = n * Y
    macs = 20 * rows * depth * width

    def projected(count):
        return [((depth, count), bf16), ((count, width), bf16), ((count, WIDE + SLIM), f32), ((count, SLIM), f32)]

    def scratch(count):
        return [pltpu.VMEM((count, depth), bf16), pltpu.VMEM((count, width), f32)]

    text = gather(trade(text_feats[0]))
    image = gather(trade(image_feats[0]))
    streams = [pltpu.VMEM((depth, width), bf16), pltpu.SemaphoreType.DMA]
    text_turned, text_emb, text_window, text_inv = call(
        text_kernel, projected(rows), scratch(rows) + streams, macs, len(text) + 1
    )(ids, *text, pltpu.with_memory_space_constraint(text_proj, pltpu.HBM))
    text_other = other_core(text_emb)
    turned_a, early, window_a, inv_a = call(image_kernel, projected(2 * n), scratch(2 * n), macs)(
        ids, *image[:2], image_proj
    )
    turned, _, window, inv = projected(2 * n)
    emb, turned_b, window_b, inv_b, slopes, slopes_turned, radial, text_radial, give, loss = call(
        slope_kernel,
        [
            ((rows, width), bf16), turned, window, inv,
            ((rows, C * rows), bf16), ((C * rows, rows), bf16), ((rows, SLIM), f32), ((rows, SLIM), f32),
            ((rows, WIDE + 2 * SLIM), f32), ((8, SLIM), f32),
        ],
        [pltpu.VMEM((2 * n, width), bf16)] + scratch(2 * n),
        macs,
    )(ids, scal, *image[2:], image_proj, early, text_emb, text_other)
    got = other_core(give)
    image_term, part, rest = call(
        grad_kernel, [((depth, WIDE + SLIM), f32), ((rows, WIDE + SLIM), f32), ((n + 8, width), f32)], (), macs
    )(
        ids, scal, turned_a, turned_b, window_a, window_b, inv_a, inv_b, emb, slopes, slopes_turned,
        radial, loss, text_emb, text_other,
    )
    packed = (XL * Z, PACK, SLIM)
    give, keep, token = call(
        sum_kernel,
        [(packed, bf16), (packed, f32), ((8, SLIM), f32)],
        [pltpu.VMEM((depth, WIDE + SLIM), f32)],
    )(ids, scal, text_turned, text_window, text_inv, text_radial, part, got, image_term)
    (outs,) = call(out_kernel, [((2 * n + TERMS, width), bf16)], (), macs)(
        scal, slopes, slopes_turned, emb, text_emb, text_other, loss, other_core(rest), token
    )
    (mine,) = call(
        add_kernel, [(packed, bf16)], [pltpu.VMEM(packed, bf16), pltpu.SemaphoreType.DMA((4,))], 0, None, pl.ANY
    )(keep, other_core(give), outs)
    outs = trade(outs)
    arrived = lax.all_to_all(mine, ("xl", "z"), 0, 0)
    (spread,) = call(spread_kernel, [((XH * Y, PACK, SLIM), bf16)])(arrived, outs)
    spread = lax.all_to_all(spread, ("xh", "y"), 0, 0)
    grad = (depth // (XL * Z * C), width), f32
    image_grad, text_grad, total, image_out, text_out = call(
        unpack_kernel, [grad, grad, ((1,), f32), ((1, n, width), bf16), ((1, n, width), bf16)]
    )(ids, spread, outs)
    return total, image_grad, text_grad, image_out, text_out


def solution(mesh):
    fine = Mesh(mesh.devices.reshape(XH, Y, XL, Z, C), AXES)
    dp, blk = ("xl", "z", "c"), ("xh", "y")
    in_specs = (P(dp, blk, None), P(dp, blk, None), P(), P(), P(), P())
    out_specs = (P(dp), P(dp, None), P(dp, None), P(dp, blk, None), P(dp, blk, None))
    return jax.shard_map(
        on_device, mesh=fine, in_specs=in_specs, out_specs=out_specs, check_vma=False
    )
```
